32 devices in a mesh: row: 8 (over z, y), col: 4 (over x, core).
Axes of the slice: x: 2, y: 2, z: 4, core: 2. Of those that a mesh axis runs over, the one named last changes fastest.
Arguments:
- lower: float32 [6, 2048, 2048], P(None, 'row', 'col'), may hold values from -0.046875 to 0.046875
- dinv: float32 [4, 2048, 2048], P(None, 'row', 'col'), as said below
- kcols: float32 [4, 2048, 2048], P(None, 'row', 'col'), may hold values from -6 to 6
- prior: float32 [2048], P('col'), may hold values from 3 to 5
Outputs:
- solved_columns: float32 [4, 2048, 2048], P(None, 'row', 'col')
- variance: float32 [2048], P('col')
The draws below stay inside these ranges and needn't reach their ends.
Inputs may be any that keep to these rules, and one draw needn't show every extreme that they name: Each block of dinv is lower triangular with a positive diagonal.
All inputs are finite; a program needn't handle non-finite values.
Results may differ from the reference program's by a relative error of at most 0.0001.
Values sent between devices are 32-bit elements; how exact they have to be, the bound alone decides.
No kernel may reach another device: no remote copies, remote signals or barrier semaphores. Data moves between devices by JAX's collectives and lax.ppermute only.
A program may use at most 64 MiB of HBM per device.

```python
import jax
import jax.numpy as jnp
from jax import lax

PANEL = 2048
STEPS = 4
CAND = 2048
PAIRS = 6
OBS = 8192


def draw_dinv(key, part):
    shape = (STEPS, PANEL, PANEL)
    noise_key = jax.random.fold_in(key, 11)
    diag_key = jax.random.fold_in(key, 23)
    noise = jax.random.normal(noise_key, shape, jnp.float32)
    diag_vals = jax.random.uniform(diag_key, shape, jnp.float32, 0.8, 1.2)
    rows_idx = jax.lax.broadcasted_iota(jnp.int32, shape, 1)
    cols_idx = jax.lax.broadcasted_iota(jnp.int32, shape, 2)
    below = (rows_idx > cols_idx).astype(jnp.float32)
    on_diag = (rows_idx == cols_idx).astype(jnp.float32)
    return below * noise * (0.5 / PANEL ** 0.5) + on_diag * diag_vals


def shard_levels(stream_key, dims, pieces, least, top_value):
    loudness, own = 1.0, jax.random.fold_in(stream_key, 6)
    for dim, blocks in pieces:
        steps = jnp.exp(jax.random.uniform(jax.random.fold_in(own, dim), (blocks,), jnp.float32, least / len(pieces), top_value / len(pieces)))
        loudness = loudness * jnp.repeat(steps, dims[dim] // blocks).reshape([-1 if axis == dim else 1 for axis in range(len(dims))])
    return loudness


def normal_values(own_key, dims, spread, bound, shards=(), kind=jnp.bfloat16):
    array = spread * jax.random.normal(own_key, dims, jnp.float32)
    if shards:
        array = array * shard_levels(own_key, dims, shards, -0.22, 0.18)
    return jnp.clip(array, -bound, bound).astype(kind)


def setup_inputs(seed: int = 0) -> dict:
    key_list = jax.random.split(jax.random.key(seed), 5)
    lower = normal_values(key_list[0], (PAIRS, PANEL, PANEL), (8 * PANEL) ** -0.5, 0.046875, ((1, 8), (2, 4)), jnp.float32)
    dinv = draw_dinv(jax.random.fold_in(key_list[4], 71), 0)
    kcols = normal_values(key_list[2], (STEPS, PANEL, CAND), 1.0, 6.0, ((1, 8), (2, 4)), jnp.float32)
    prior = jnp.clip(3.0 + 2.0 * jax.random.uniform(key_list[3], (CAND,), jnp.float32) ** shard_levels(key_list[3], (CAND,), ((0, 4),), -0.2, 0.2), 3.0, 5.0)
    return {"lower": lower, "dinv": dinv, "kcols": kcols, "prior": prior}


def reference(lower, dinv, kcols, prior):
    solved = []
    for segment_now in range(STEPS):
        residual = kcols[segment_now]
        for earlier in range(segment_now):
            residual = residual - jnp.dot(lower[segment_now * (segment_now - 1) // 2 + earlier], solved[earlier], precision=lax.Precision.HIGHEST, preferred_element_type=jnp.float32)
        solved.append(jnp.dot(dinv[segment_now], residual, precision=lax.Precision.HIGHEST, preferred_element_type=jnp.float32))
    solution = jnp.stack(solved)
    variance = prior - jnp.sum(solution * solution, axis=(0, 1)) / OBS
    return solution, variance
```

```python
import jax
import jax.numpy as jnp
from jax import lax
from jax.sharding import PartitionSpec as P

STREAMS = 1


def mul(a, b):
    return jnp.dot(a, b, precision=lax.Precision.HIGH, preferred_element_type=jnp.float32)


def make_body(rows, cols, streams):
    layers = rows // 2
    ring = [(r, (r + 2) % rows) for r in range(rows)]
    pair = [(r, r ^ 1) for r in range(rows)]

    def body(lower, dinv, kcols, prior):
        segments, height, breadth = kcols.shape
        observed = segments * height * rows
        position = lax.axis_index("row")
        column = lax.axis_index("col")
        layer, parity = position // 2, position % 2
        per_col = layers // cols

        def spread_factor(block):
            split = block.reshape(height, per_col, 2, height)
            even = split[:, :, 0, :].reshape(height, per_col * height)
            odd = split[:, :, 1, :].reshape(height, per_col * height)
            mine = jnp.where(parity == 0, even, odd)
            theirs = jnp.where(parity == 0, odd, even)
            piece = jnp.concatenate([mine, lax.ppermute(theirs, "row", pair)], axis=0)
            bit = cols // 2
            while bit:
                swap = [(c, c ^ bit) for c in range(cols)]
                piece = jnp.concatenate([piece, lax.ppermute(piece, "col", swap)], axis=1)
                bit //= 2
            return piece

        def place(source):
            slot = column ^ (source // per_col)
            order, bit, weight = 0, cols // 2, 1
            while bit:
                order = order + jnp.where((slot & bit) != 0, weight, 0)
                bit //= 2
                weight *= 2
            return (order * per_col + source % per_col) * height

        def gather(panel):
            whole = jnp.zeros((layers * height, panel.shape[1]), panel.dtype)
            moving = panel
            for hop in range(layers):
                source = (layer - hop) % layers
                whole = lax.dynamic_update_slice(whole, moving, (place(source), 0))
                if hop + 1 < layers:
                    moving = lax.ppermute(moving, "row", ring)
            return whole

        def factor(s, t):
            return dinv[s] if s == t else lower[s * (s - 1) // 2 + t]

        factors = {}
        for s in range(segments):
            factors[s, s] = spread_factor(factor(s, s))
            for u in range(s + 1, segments):
                factors[u, s] = spread_factor(factor(u, s))

        width = breadth // streams
        residual = [kcols[0, :, i * width : (i + 1) * width] for i in range(streams)]
        sums = [[None] * segments for i in range(streams)]
        solved = [[] for i in range(streams)]
        for s in range(segments):
            for i in range(streams):
                whole = gather(residual[i])
                both = factors[s, s]
                other = lax.ppermute(mul(both[height:], whole), "row", pair)
                solved[i].append(mul(both[:height], whole) + other)
            if s + 1 == segments:
                break
            for i in range(streams):
                whole = gather(solved[i][s])
                for u in range(s + 1, segments):
                    own = mul(factors[u, s][:height], whole)
                    away = mul(factors[u, s][height:], whole)
                    if sums[i][u] is not None:
                        own, away = own + sums[i][u][0], away + sums[i][u][1]
                    sums[i][u] = (own, away)
                own, away = sums[i][s + 1]
                other = lax.ppermute(away, "row", pair)
                residual[i] = kcols[s + 1, :, i * width : (i + 1) * width] - own - other
        solution = jnp.stack(
            [jnp.concatenate([solved[i][s] for i in range(streams)], axis=1) for s in range(segments)]
        )
        totals = jnp.sum(solution * solution, axis=(0, 1))
        bit = 1
        while bit < rows:
            totals = totals + lax.ppermute(totals, "row", [(r, r ^ bit) for r in range(rows)])
            bit *= 2
        variance = prior - totals / observed
        return (solution, variance)

    return body


def solution(mesh):
    body = make_body(mesh.shape["row"], mesh.shape["col"], STREAMS)
    in_specs = (P(None, "row", "col"), P(None, "row", "col"), P(None, "row", "col"), P("col"))
    out_specs = (P(None, "row", "col"), P("col"))
    return jax.shard_map(body, mesh=mesh, in_specs=in_specs, out_specs=out_specs, check_vma=False)
```

```python
import functools

import jax
import jax.numpy as jnp
from jax import lax
from jax.experimental import pallas as pl
from jax.experimental.pallas import tpu as pltpu
from jax.sharding import PartitionSpec as P

STREAMS = 2
LAYERS = 4
dot = functools.partial(jnp.dot, preferred_element_type=jnp.float32)


def halves(value):
    high = value.astype(jnp.bfloat16)
    return high, (value - high.astype(jnp.float32)).astype(jnp.bfloat16)


def product_kernel(layers, sign, by_xor, pieces, based, *refs):
    factor, panels, refs = refs[:pieces], refs[pieces : pieces + layers], refs[pieces + layers :]
    bases, (own, away, fh, fl, xh, xl) = refs[:-6], refs[-6:]
    height = panels[0].shape[0]
    layer = lax.axis_index("row") // 2
    column = lax.axis_index("col")
    for hop, ref in enumerate(panels):
        source = lax.rem(layer + layers - hop, layers)
        slot = jnp.bitwise_xor(source, column) if by_xor else source
        start = pl.multiple_of(slot * height, height)
        xh[pl.ds(start, height), :], xl[pl.ds(start, height), :] = halves(ref[...])
    for half, out in ((1, away), (0, own)):
        for slot in range(layers):
            block = factor[slot][half] if pieces > 1 else factor[0][slot, 0, half]
            section = slice(slot * height, (slot + 1) * height)
            fh[:, section], fl[:, section] = halves(block)
        total = dot(fl[...], xh[...]) + dot(fh[...], xl[...]) + dot(fh[...], xh[...])
        total = total if sign > 0 else -total
        out[...] = bases[half][...] + total if based[half] else total


def after(value, *events):
    return lax.optimization_barrier((value, *events))[0]


def make_body(rows, cols, streams):
    layers = rows // 2
    pair = [(r, r ^ 1) for r in range(rows)]

    ring = [(r, (r + 2) % rows) for r in range(rows)]

    def body(lower, dinv, kcols, prior):
        segments, height, breadth = kcols.shape
        observed = segments * height * rows
        width = breadth // streams
        layer, parity = lax.axis_index("row") // 2, lax.axis_index("row") % 2
        column = lax.axis_index("col")
        vmem = functools.partial(pltpu.CompilerParams, vmem_limit_bytes=24 * 2**20)

        def swap(value):
            return lax.ppermute(value, "row", pair)

        def cross(value, bits):
            return lax.ppermute(value, "col", [(c, c ^ bits) for c in range(cols)])

        def by_parity(blocks):
            even, odd = blocks[..., :height], blocks[..., height:]
            return jnp.where(parity == 0, even, odd), jnp.where(parity == 0, odd, even)

        def ring_of(panels, waits={}):
            slots = [[panel] for panel in panels]
            for hop in range(1, layers):
                for i in range(streams):
                    value = slots[i][-1]
                    if (i, hop) in waits:
                        value = after(value, *waits[i, hop])
                    slots[i].append(lax.ppermute(value, "row", ring))
            return slots, [[stream[hop] for stream in slots] for hop in range(layers)]

        def block_spec(shape):
            return pl.BlockSpec(shape, lambda i: (0,) * len(shape))

        def product(factor, panels, bases=(), sign=1):
            if isinstance(factor, list):
                pieces, specs = factor, [block_spec(piece.shape) for piece in factor]
            else:
                pieces, index = [factor[0]], factor[1]
                specs = [pl.BlockSpec((cols, 1, 2, height, height), lambda i: (0, index, 0, 0, 0))]
            wide = panels[0].shape[1]
            depth = layers * height
            shape = jax.ShapeDtypeStruct((height, wide), jnp.float32)
            based = (len(bases) > 0, len(bases) > 1)
            return pl.pallas_call(
                functools.partial(product_kernel, layers, sign, len(pieces) > 1, len(pieces), based),
                grid=(1,),
                out_shape=[shape] * 2,
                in_specs=specs + [block_spec((height, wide))] * (layers + len(bases)),
                out_specs=[block_spec((height, wide))] * 2,
                scratch_shapes=[pltpu.VMEM((height, depth), jnp.bfloat16)] * 2
                + [pltpu.VMEM((depth, wide), jnp.bfloat16)] * 2,
                compiler_params=pltpu.CompilerParams(vmem_limit_bytes=24 * 2**20),
                cost_estimate=pl.CostEstimate(
                    flops=12 * height * depth * wide,
                    bytes_accessed=4 * (2 * height * depth + (layers + 2 + len(bases)) * height * wide),
                    transcendentals=0,
                ),
            )(*pieces, *panels, *bases)

        cut = [slice(i * width, (i + 1) * width) for i in range(streams)]
        sums = [[(kcols[s, :, c],) for s in range(segments)] for c in cut]
        solved = [[None] * segments for i in range(streams)]

        def block(s, t):
            return dinv[s] if s == t else lower[s * (s - 1) // 2 + t]

        def exchange(keys, start, use):
            mine, theirs = by_parity(jnp.stack([block(s, t) for s, t in keys]))
            got = swap(after(theirs, *start) if start else theirs)
            return jnp.stack([mine, after(got, *use)], axis=-3), got

        found = {}

        def fetch(keys, start, use):
            piece, got = exchange(keys, start, use)
            whole = lax.all_gather(piece, "col", axis=0)
            for index, key in enumerate(keys):
                found[key] = (whole, index)

        firsts = [kcols[0, :, c] for c in cut]
        one = lax.ppermute(firsts[0], "row", ring)
        piece, got = exchange([(0, 0)], [], [one])
        near = cross(piece[0], 1)
        beside = cross(piece[0], 2)
        far = cross(after(beside, near), 1)
        found[0, 0] = [piece[0], near, beside, far]
        slots, hops = ring_of(firsts, {(streams - 1, 2): [near], (streams - 1, 3): [far]})
        fetch([(1, 0)], [got], hops[2])
        fetch([(1, 1), (2, 0), (2, 1)], [got, *hops[2]], hops[3])
        for s in range(segments):
            for i in range(streams):
                own, away = product(found[s, s], slots[i])
                solved[i][s] = own + swap(away)
            if s + 1 == segments:
                break
            panels, after_x = ring_of([solved[i][s] for i in range(streams)])
            if s == 0:
                fetch([(2, 2), (3, 0), (3, 1), (3, 2), (3, 3)], after_x[0], after_x[3])
            residuals = []
            for i in range(streams):
                own, away = product(found[s + 1, s], panels[i], sums[i][s + 1], -1)
                residuals.append(own + swap(away))
            early = []
            if s == 0:
                for i in range(streams):
                    sums[i][2] = product(found[2, 0], panels[i], sums[i][2], -1)
                    early.append(sums[i][2][0])
            if s == 1:
                for i in range(streams):
                    sums[i][3] = product(found[3, 0], first_panels[i], sums[i][3], -1)
                    sums[i][3] = product(found[3, 1], panels[i], sums[i][3], -1)
                    early.append(sums[i][3][0])
            first_panels = panels
            slots, hops = ring_of(residuals, {(streams - 1, 3): early} if early else {})
        solution = jnp.stack(
            [jnp.concatenate([solved[i][s] for i in range(streams)], axis=1) for s in range(segments)]
        )
        totals = jnp.sum(solution * solution, axis=(0, 1))
        bit = 1
        while bit < rows:
            totals = totals + lax.ppermute(totals, "row", [(r, r ^ bit) for r in range(rows)])
            bit *= 2
        variance = prior - totals / observed
        return (solution, variance)

    return body


def whole_body(lower, dinv, kcols, prior):
    segments = kcols.shape[0]
    high = functools.partial(dot, precision=lax.Precision.HIGHEST)
    spread, solved = [], []
    for s in range(segments):
        residual = kcols[s]
        for t in range(s):
            block = lax.all_gather(lower[s * (s - 1) // 2 + t], "col", axis=1, tiled=True)
            residual = residual - high(block, spread[t])
        whole = lax.all_gather(residual, "row", axis=0, tiled=True)
        answer = high(lax.all_gather(dinv[s], "col", axis=1, tiled=True), whole)
        solved.append(answer)
        if s + 1 < segments:
            spread.append(lax.all_gather(answer, "row", axis=0, tiled=True))
    solution = jnp.stack(solved)
    totals = lax.psum(jnp.sum(solution * solution, axis=(0, 1)), "row")
    return solution, prior - totals / (segments * dinv.shape[2] * lax.axis_size("col"))


def solution(mesh):
    rows, cols = mesh.shape["row"], mesh.shape["col"]
    if rows == 2 * LAYERS and cols == LAYERS:
        body = make_body(rows, cols, STREAMS)
    else:
        body = whole_body
    in_specs = (P(None, "row", "col"), P(None, "row", "col"), P(None, "row", "col"), P("col"))
    out_specs = (P(None, "row", "col"), P("col"))
    return jax.shard_map(body, mesh=mesh, in_specs=in_specs, out_specs=out_specs, check_vma=False)
```

```python
import functools

import jax
import jax.numpy as jnp
from jax import lax
from jax.experimental import pallas as pl
from jax.experimental.pallas import tpu as pltpu
from jax.sharding import PartitionSpec as P

STREAMS = 2
LAYERS = 4
dot = functools.partial(jnp.dot, preferred_element_type=jnp.float32)


def halves(value):
    high = value.astype(jnp.bfloat16)
    return high, (value - high.astype(jnp.float32)).astype(jnp.bfloat16)


def product_kernel(layers, sign, by_xor, pieces, based, *refs):
    factor, panels, refs = refs[:pieces], refs[pieces : pieces + layers], refs[pieces + layers :]
    bases, (own, away, fh, fl, xh, xl) = refs[:-6], refs[-6:]
    height = panels[0].shape[0]
    layer = lax.axis_index("row") // 2
    column = lax.axis_index("col")
    for hop, ref in enumerate(panels):
        source = lax.rem(layer + layers - hop, layers)
        slot = jnp.bitwise_xor(source, column) if by_xor else source
        start = pl.multiple_of(slot * height, height)
        xh[pl.ds(start, height), :], xl[pl.ds(start, height), :] = halves(ref[...])
    for half, out in ((1, away), (0, own)):
        for slot in range(layers):
            block = factor[slot][half] if pieces > 1 else factor[0][slot, half, 0]
            section = slice(slot * height, (slot + 1) * height)
            fh[:, section], fl[:, section] = halves(block)
        total = dot(fl[...], xh[...]) + dot(fh[...], xl[...]) + dot(fh[...], xh[...])
        total = total if sign > 0 else -total
        out[...] = bases[half][...] + total if based[half] else total


def after(value, *events):
    return lax.optimization_barrier((value, *events))[0]


def make_body(rows, cols, streams):
    layers = rows // 2
    pair = [(r, r ^ 1) for r in range(rows)]

    ring = [(r, (r + 2) % rows) for r in range(rows)]
    climb = [[(r, r + 2) for r in range(2 * hop, rows - 2)] for hop in range(layers - 1)]
    circle = [ring] * (layers - 1)

    def body(lower, dinv, kcols, prior):
        segments, height, breadth = kcols.shape
        observed = segments * height * rows
        width = breadth // streams
        layer, parity = lax.axis_index("row") // 2, lax.axis_index("row") % 2
        column = lax.axis_index("col")
        vmem = functools.partial(pltpu.CompilerParams, vmem_limit_bytes=24 * 2**20)

        def swap(value):
            return lax.ppermute(value, "row", pair)

        def cross(value, bits):
            return lax.ppermute(value, "col", [(c, c ^ bits) for c in range(cols)])

        def by_parity(blocks):
            even, odd = blocks[..., :height], blocks[..., height:]
            return jnp.where(parity == 0, even, odd), jnp.where(parity == 0, odd, even)

        def ring_of(panels, route, waits={}):
            slots = [[panel] for panel in panels]
            for hop in range(1, layers):
                for i in range(streams):
                    value = slots[i][-1]
                    if (i, hop) in waits:
                        value = after(value, *waits[i, hop])
                    slots[i].append(lax.ppermute(value, "row", route[hop - 1]))
            return slots, [[stream[hop] for stream in slots] for hop in range(layers)]

        def block_spec(shape):
            return pl.BlockSpec(shape, lambda i: (0,) * len(shape))

        def product(factor, panels, bases=(), sign=1):
            if isinstance(factor, list):
                pieces, specs = factor, [block_spec(piece.shape) for piece in factor]
            else:
                pieces, index = [factor[0]], factor[1]
                specs = [pl.BlockSpec((cols, 2, 1, height, height), lambda i: (0, 0, index, 0, 0))]
            wide = panels[0].shape[1]
            depth = layers * height
            shape = jax.ShapeDtypeStruct((height, wide), jnp.float32)
            based = (len(bases) > 0, len(bases) > 1)
            return pl.pallas_call(
                functools.partial(product_kernel, layers, sign, len(pieces) > 1, len(pieces), based),
                grid=(1,),
                out_shape=[shape] * 2,
                in_specs=specs + [block_spec((height, wide))] * (layers + len(bases)),
                out_specs=[block_spec((height, wide))] * 2,
                scratch_shapes=[pltpu.VMEM((height, depth), jnp.bfloat16)] * 2
                + [pltpu.VMEM((depth, wide), jnp.bfloat16)] * 2,
                compiler_params=pltpu.CompilerParams(vmem_limit_bytes=24 * 2**20),
                cost_estimate=pl.CostEstimate(
                    flops=12 * height * depth * wide,
                    bytes_accessed=4 * (2 * height * depth + (layers + 2 + len(bases)) * height * wide),
                    transcendentals=0,
                ),
            )(*pieces, *panels, *bases)

        cut = [slice(i * width, (i + 1) * width) for i in range(streams)]
        sums = [[(kcols[s, :, c],) for s in range(segments)] for c in cut]
        solved = [[None] * segments for i in range(streams)]

        def block(s, t):
            return dinv[s] if s == t else lower[s * (s - 1) // 2 + t]

        def exchange(keys, start, use):
            mine, theirs = by_parity(jnp.stack([block(s, t) for s, t in keys]))
            got = swap(after(theirs, *start) if start else theirs)
            return jnp.stack([mine, after(got, *use)]), got

        found = {}

        def fetch(keys, start, use):
            piece, got = exchange(keys, start, use)
            whole = lax.all_gather(piece, "col", axis=0)
            for index, key in enumerate(keys):
                found[key] = (whole, index)

        firsts = [kcols[0, :, c] for c in cut]
        slots, hops = ring_of(firsts, climb)
        fetch([(0, 0)], [], hops[1][:1])
        fetch([(1, 0)], hops[1], hops[2])
        fetch([(1, 1)], hops[2][:1], hops[3])
        for s in range(segments):
            for i in range(streams):
                own, away = product(found[s, s], slots[i])
                solved[i][s] = own + swap(away)
            if s + 1 == segments:
                break
            panels, after_x = ring_of([solved[i][s] for i in range(streams)], circle)
            if s == 0:
                fetch([(2, 0), (2, 1), (2, 2)], after_x[0], after_x[2])
            residuals = []
            for i in range(streams):
                own, away = product(found[s + 1, s], panels[i], sums[i][s + 1], -1)
                residuals.append(own + swap(away))
            early = []
            if s == 0:
                for i in range(streams):
                    sums[i][2] = product(found[2, 0], panels[i], sums[i][2], -1)
                    early.append(sums[i][2][0])
            if s == 1:
                for i in range(streams):
                    sums[i][3] = product(found[3, 0], first_panels[i], sums[i][3], -1)
                    sums[i][3] = product(found[3, 1], panels[i], sums[i][3], -1)
                    early.append(sums[i][3][0])
            first_panels = panels
            slots, hops = ring_of(residuals, climb)
            if s == 0:
                fetch([(3, 0), (3, 1), (3, 2), (3, 3)], hops[0], hops[2])
        solution = jnp.stack(
            [jnp.concatenate([solved[i][s] for i in range(streams)], axis=1) for s in range(segments)]
        )
        totals = jnp.sum(solution * solution, axis=(0, 1))
        bit = 1
        while bit < rows:
            totals = totals + lax.ppermute(totals, "row", [(r, r ^ bit) for r in range(rows)])
            bit *= 2
        variance = prior - totals / observed
        return (solution, variance)

    return body


def whole_body(lower, dinv, kcols, prior):
    segments = kcols.shape[0]
    high = functools.partial(dot, precision=lax.Precision.HIGHEST)
    spread, solved = [], []
    for s in range(segments):
        residual = kcols[s]
        for t in range(s):
            block = lax.all_gather(lower[s * (s - 1) // 2 + t], "col", axis=1, tiled=True)
            residual = residual - high(block, spread[t])
        whole = lax.all_gather(residual, "row", axis=0, tiled=True)
        answer = high(lax.all_gather(dinv[s], "col", axis=1, tiled=True), whole)
        solved.append(answer)
        if s + 1 < segments:
            spread.append(lax.all_gather(answer, "row", axis=0, tiled=True))
    solution = jnp.stack(solved)
    totals = lax.psum(jnp.sum(solution * solution, axis=(0, 1)), "row")
    return solution, prior - totals / (segments * dinv.shape[2] * lax.axis_size("col"))


def solution(mesh):
    rows, cols = mesh.shape["row"], mesh.shape["col"]
    if rows == 2 * LAYERS and cols == LAYERS:
        body = make_body(rows, cols, STREAMS)
    else:
        body = whole_body
    in_specs = (P(None, "row", "col"), P(None, "row", "col"), P(None, "row", "col"), P("col"))
    out_specs = (P(None, "row", "col"), P("col"))
    return jax.shard_map(body, mesh=mesh, in_specs=in_specs, out_specs=out_specs, check_vma=False)
```

```python
import functools

import jax
import jax.numpy as jnp
from jax import lax
from jax.experimental import pallas as pl
from jax.experimental.pallas import tpu as pltpu
from jax.sharding import PartitionSpec as P

STREAMS = 2
LAYERS = 4
dot = functools.partial(jnp.dot, preferred_element_type=jnp.float32)


def halves(value):
    high = value.astype(jnp.bfloat16)
    return high, (value - high.astype(jnp.float32)).astype(jnp.bfloat16)


def product_kernel(layers, sign, by_xor, pieces, based, *refs):
    factor, panels, refs = refs[:pieces], refs[pieces : pieces + layers], refs[pieces + layers :]
    bases, (own, away, fh, fl, xh, xl) = refs[:-6], refs[-6:]
    height = panels[0].shape[0]
    layer = lax.axis_index("row") // 2
    column = lax.axis_index("col")
    for hop, ref in enumerate(panels):
        source = lax.rem(layer + layers - hop, layers)
        slot = jnp.bitwise_xor(source, column) if by_xor else source
        start = pl.multiple_of(slot * height, height)
        xh[pl.ds(start, height), :], xl[pl.ds(start, height), :] = halves(ref[...])
    for half, out in ((1, away), (0, own)):
        for slot in range(layers):
            block = factor[slot][half] if pieces > 1 else factor[0][slot, half, 0]
            section = slice(slot * height, (slot + 1) * height)
            fh[:, section], fl[:, section] = halves(block)
        total = dot(fl[...], xh[...]) + dot(fh[...], xl[...]) + dot(fh[...], xh[...])
        total = total if sign > 0 else -total
        out[...] = bases[half][...] + total if based[half] else total


def after(value, *events):
    return lax.optimization_barrier((value, *events))[0]


def make_body(rows, cols, streams):
    layers = rows // 2
    pair = [(r, r ^ 1) for r in range(rows)]

    ring = [(r, (r + 2) % rows) for r in range(rows)]
    climb = [[(r, r + 2) for r in range(2 * hop, rows - 2)] for hop in range(layers - 1)]
    circle = [ring] * (layers - 1)

    def body(lower, dinv, kcols, prior):
        segments, height, breadth = kcols.shape
        observed = segments * height * rows
        width = breadth // streams
        layer, parity = lax.axis_index("row") // 2, lax.axis_index("row") % 2
        column = lax.axis_index("col")
        vmem = functools.partial(pltpu.CompilerParams, vmem_limit_bytes=24 * 2**20)

        def swap(value):
            return lax.ppermute(value, "row", pair)

        def cross(value, bits):
            return lax.ppermute(value, "col", [(c, c ^ bits) for c in range(cols)])

        def by_parity(blocks):
            even, odd = blocks[..., :height], blocks[..., height:]
            return jnp.where(parity == 0, even, odd), jnp.where(parity == 0, odd, even)

        def ring_of(panels, route, waits={}):
            slots = [[panel] for panel in panels]
            for hop in range(1, layers):
                for i in range(streams):
                    value = slots[i][-1]
                    if (i, hop) in waits:
                        value = after(value, *waits[i, hop])
                    slots[i].append(lax.ppermute(value, "row", route[hop - 1]))
            return slots, [[stream[hop] for stream in slots] for hop in range(layers)]

        def block_spec(shape):
            return pl.BlockSpec(shape, lambda i: (0,) * len(shape))

        def product(factor, panels, bases=(), sign=1):
            if isinstance(factor, list):
                pieces, specs = factor, [block_spec(piece.shape) for piece in factor]
            else:
                pieces, index = [factor[0]], factor[1]
                specs = [pl.BlockSpec((cols, 2, 1, height, height), lambda i: (0, 0, index, 0, 0))]
            wide = panels[0].shape[1]
            depth = layers * height
            shape = jax.ShapeDtypeStruct((height, wide), jnp.float32)
            based = (len(bases) > 0, len(bases) > 1)
            return pl.pallas_call(
                functools.partial(product_kernel, layers, sign, len(pieces) > 1, len(pieces), based),
                grid=(1,),
                out_shape=[shape] * 2,
                in_specs=specs + [block_spec((height, wide))] * (layers + len(bases)),
                out_specs=[block_spec((height, wide))] * 2,
                scratch_shapes=[pltpu.VMEM((height, depth), jnp.bfloat16)] * 2
                + [pltpu.VMEM((depth, wide), jnp.bfloat16)] * 2,
                compiler_params=pltpu.CompilerParams(vmem_limit_bytes=24 * 2**20),
                cost_estimate=pl.CostEstimate(
                    flops=12 * height * depth * wide,
                    bytes_accessed=4 * (2 * height * depth + (layers + 2 + len(bases)) * height * wide),
                    transcendentals=0,
                ),
            )(*pieces, *panels, *bases)

        cut = [slice(i * width, (i + 1) * width) for i in range(streams)]
        sums = [[(kcols[s, :, c],) for s in range(segments)] for c in cut]
        solved = [[None] * segments for i in range(streams)]

        def block(s, t):
            return dinv[s] if s == t else lower[s * (s - 1) // 2 + t]

        def exchange(keys, start, use):
            mine, theirs = by_parity(jnp.stack([block(s, t) for s, t in keys]))
            got = swap(after(theirs, *start) if start else theirs)
            return jnp.stack([mine, after(got, *use)]), got

        found = {}

        def fetch(keys, start, use):
            piece, got = exchange(keys, start, use)
            whole = lax.all_gather(piece, "col", axis=0)
            for index, key in enumerate(keys):
                found[key] = (whole, index)

        firsts = [kcols[0, :, c] for c in cut]
        slots, hops = ring_of(firsts, climb)
        fetch([(0, 0)], [], hops[1][:1])
        fetch([(1, 0)], hops[1], hops[2])
        fetch([(1, 1)], hops[2][:1], hops[3])
        for s in range(segments):
            for i in range(streams):
                own, away = product(found[s, s], slots[i])
                solved[i][s] = own + swap(away)
            if s + 1 == segments:
                break
            panels, after_x = ring_of([solved[i][s] for i in range(streams)], circle)
            if s == 0:
                fetch([(2, 0), (2, 1), (2, 2)], after_x[0], after_x[2])
            residuals = []
            for i in range(streams):
                own, away = product(found[s + 1, s], panels[i], sums[i][s + 1], -1)
                residuals.append(own + swap(away))
            early = []
            if s == 0:
                for i in range(streams):
                    sums[i][2] = product(found[2, 0], panels[i], sums[i][2], -1)
                    early.append(sums[i][2][0])
            if s == 1:
                for i in range(streams):
                    sums[i][3] = product(found[3, 0], first_panels[i], sums[i][3], -1)
                    sums[i][3] = product(found[3, 1], panels[i], sums[i][3], -1)
                    early.append(sums[i][3][0])
            first_panels = panels
            slots, hops = ring_of(residuals, climb)
            if s == 0:
                fetch([(3, 0), (3, 1), (3, 2), (3, 3)], hops[1], hops[3])
        solution = jnp.stack(
            [jnp.concatenate([solved[i][s] for i in range(streams)], axis=1) for s in range(segments)]
        )
        totals = jnp.concatenate(
            [sum(jnp.sum(panel * panel, axis=0) for panel in solved[i]) for i in range(streams)]
        )
        bit = rows // 2
        while bit:
            totals = totals + lax.ppermute(totals, "row", [(r, r ^ bit) for r in range(rows)])
            bit //= 2
        variance = prior - totals / observed
        return (solution, variance)

    return body


def whole_body(lower, dinv, kcols, prior):
    segments = kcols.shape[0]
    high = functools.partial(dot, precision=lax.Precision.HIGHEST)
    spread, solved = [], []
    for s in range(segments):
        residual = kcols[s]
        for t in range(s):
            block = lax.all_gather(lower[s * (s - 1) // 2 + t], "col", axis=1, tiled=True)
            residual = residual - high(block, spread[t])
        whole = lax.all_gather(residual, "row", axis=0, tiled=True)
        answer = high(lax.all_gather(dinv[s], "col", axis=1, tiled=True), whole)
        solved.append(answer)
        if s + 1 < segments:
            spread.append(lax.all_gather(answer, "row", axis=0, tiled=True))
    solution = jnp.stack(solved)
    totals = lax.psum(jnp.sum(solution * solution, axis=(0, 1)), "row")
    return solution, prior - totals / (segments * dinv.shape[2] * lax.axis_size("col"))


def solution(mesh):
    rows, cols = mesh.shape["row"], mesh.shape["col"]
    if rows == 2 * LAYERS and cols == LAYERS:
        body = make_body(rows, cols, STREAMS)
    else:
        body = whole_body
    in_specs = (P(None, "row", "col"), P(None, "row", "col"), P(None, "row", "col"), P("col"))
    out_specs = (P(None, "row", "col"), P("col"))
    return jax.shard_map(body, mesh=mesh, in_specs=in_specs, out_specs=out_specs, check_vma=False)
```
